32 devices in a mesh: pipe: 2 (over x), dp: 8 (over z, y), tensor: 2 (over core).
Axes of the slice: x: 2, y: 2, z: 4, core: 2. Of those that a mesh axis runs over, the one named last changes fastest.
Arguments:
- tokens: bfloat16 [1024, 2048], P('dp'), may hold values from -6 to 6
- cotangent: bfloat16 [1024, 2048], P('dp'), may hold values from -6 to 6
- attn_gain: bfloat16 [2, 2048], P('pipe', 'dp'), may hold values from 0.5 to 1.5
- w_query: bfloat16 [2, 2048, 2048], P('pipe', 'dp', 'tensor'), may hold values from -0.125 to 0.125
- w_key: bfloat16 [2, 2048, 512], P('pipe', 'dp', 'tensor'), may hold values from -0.125 to 0.125
- w_value: bfloat16 [2, 2048, 512], P('pipe', 'dp', 'tensor'), may hold values from -0.125 to 0.125
- w_out: bfloat16 [2, 2048, 2048], P('pipe', 'tensor', 'dp'), may hold values from -0.375 to 0.375
- mlp_gain: bfloat16 [2, 2048], P('pipe', 'dp'), may hold values from 0.5 to 1.5
- w_gate: bfloat16 [2, 2048, 8192], P('pipe', 'dp', 'tensor'), may hold values from -0.125 to 0.125
- w_up: bfloat16 [2, 2048, 8192], P('pipe', 'dp', 'tensor'), may hold values from -0.125 to 0.125
- w_down: bfloat16 [2, 8192, 2048], P('pipe', 'tensor', 'dp'), may hold values from -0.0625 to 0.0625
Outputs:
- activations: bfloat16 [2, 1024, 2048], P('pipe', 'dp')
- input_grads: float32 [2, 1024, 2048], P('pipe', 'dp')
- grad_attn_gain: float32 [2, 2048], P('pipe', 'dp')
- grad_query: float32 [2, 2048, 2048], P('pipe', 'dp', 'tensor')
- grad_key: float32 [2, 2048, 512], P('pipe', 'dp', 'tensor')
- grad_value: float32 [2, 2048, 512], P('pipe', 'dp', 'tensor')
- grad_out: float32 [2, 2048, 2048], P('pipe', 'tensor', 'dp')
- grad_mlp_gain: float32 [2, 2048], P('pipe', 'dp')
- grad_gate: float32 [2, 2048, 8192], P('pipe', 'dp', 'tensor')
- grad_up: float32 [2, 2048, 8192], P('pipe', 'dp', 'tensor')
- grad_down: float32 [2, 8192, 2048], P('pipe', 'tensor', 'dp')
The draws below stay inside these ranges and needn't reach their ends.
All inputs are finite; a program needn't handle non-finite values.
Results may differ from the reference program's by a relative error of at most 0.03.
Values may be sent and summed in bfloat16 or wider, within the bound.
No kernel may reach another device: no remote copies, remote signals or barrier semaphores. Data moves between devices by JAX's collectives and lax.ppermute only.
A program may use at most 512 MiB of HBM per device.

```python
import jax
import jax.numpy as jnp
from jax import lax

D = 2048
FF = 8192
QH = 32
KVH = 8
HEAD = 64
SEQ = 128
TOKENS = 1024
N_DP = 8


def strengthened(drawn, rng, source, target, blocks, factor):
    owner, partner = [(jnp.arange(drawn.shape[position]) // (drawn.shape[position] // blocks)).reshape([-1 if axis == position else 1 for axis in range(drawn.ndim)]) for position in (source, target)]
    chosen = jax.random.permutation(rng, blocks)[partner]
    strong = (owner == chosen) | (owner == (partner + blocks // 2) % blocks)
    return jnp.where(strong, factor * drawn, drawn)


def levels(stream_key, shape, cuts, least, high):
    def one(dim, shards_of):
        steps = jax.random.uniform(jax.random.fold_in(jax.random.fold_in(stream_key, 6), dim), (shards_of,), jnp.float32, least / len(cuts), high / len(cuts))
        return jnp.repeat(jnp.exp(steps), shape[dim] // shards_of).reshape((-1,) + (1,) * (len(shape) - dim - 1))

    level = one(*cuts[0])
    for cut in cuts[1:]:
        level = level * one(*cut)
    return level


def normal_values(stream_key, dims, width, most, pieces=(), kind=jnp.bfloat16):
    values = width * jax.random.normal(stream_key, dims, jnp.float32)
    if pieces:
        values = values * levels(stream_key, dims, pieces, -0.22, 0.18)
    return jnp.clip(values, -most, most).astype(kind)


def heavy_noise(key, extent, scale, reach, shards, heavy, kind=jnp.bfloat16):
    result = scale * jax.random.normal(key, extent, jnp.float32)
    if shards:
        result = result * levels(key, extent, shards, -0.22, 0.18)
    return jnp.clip(strengthened(result, jax.random.fold_in(key, 3), *heavy), -reach, reach).astype(kind)


def setup_inputs(seed: int = 0) -> dict:
    key_of = jax.random.split(jax.random.key(seed), 12)
    return {
        "tokens": heavy_noise(key_of[0], (TOKENS, D), 1.0, 6.0, ((0, 8),), (0, 1, 8, 2.0)),
        "cotangent": heavy_noise(key_of[1], (TOKENS, D), 1.0, 6.0, ((0, 8),), (0, 1, 8, 2.0)),
        "attn_gain": jnp.clip(1.0 + 0.1 * jax.random.normal(key_of[2], (2, D), jnp.float32), 0.5, 1.5).astype(jnp.bfloat16),
        "w_query": normal_values(key_of[3], (2, D, QH * HEAD), D ** -0.5, 0.125, ((0, 2), (1, 8), (2, 2))),
        "w_key": normal_values(key_of[4], (2, D, KVH * HEAD), D ** -0.5, 0.125, ((0, 2), (1, 8), (2, 2))),
        "w_value": normal_values(key_of[5], (2, D, KVH * HEAD), D ** -0.5, 0.125, ((0, 2), (1, 8), (2, 2))),
        "w_out": normal_values(key_of[6], (2, QH * HEAD, D), (QH * HEAD // 8) ** -0.5, 0.375, ((0, 2), (1, 2), (2, 8))),
        "mlp_gain": jnp.clip(1.0 + 0.1 * jax.random.normal(key_of[7], (2, D), jnp.float32), 0.5, 1.5).astype(jnp.bfloat16),
        "w_gate": normal_values(key_of[8], (2, D, FF), D ** -0.5, 0.125, ((0, 2), (1, 8), (2, 2))),
        "w_up": normal_values(key_of[9], (2, D, FF), D ** -0.5, 0.125, ((0, 2), (1, 8), (2, 2))),
        "w_down": normal_values(key_of[10], (2, FF, D), FF ** -0.5, 0.0625, ((0, 2), (1, 2), (2, 8))),
    }


@jax.custom_vjp
def low(v):
    return lax.optimization_barrier(v.astype(jnp.bfloat16)).astype(jnp.float32)

@jax.custom_vjp
def low_back(v):
    return v

def low_keep(v):
    return (low(v), None)

def low_pass(kept, grad):
    return (grad,)

def back_keep(v):
    return (v, None)

def back_low(kept, grad):
    return (low(grad),)
low.defvjp(low_keep, low_pass)
low_back.defvjp(back_keep, back_low)
eps = 1e-05
theta = 500000.0

def rope_angles(first_row, row_count, head_size):
    positions = (first_row + jnp.arange(row_count, dtype=jnp.int32)).astype(jnp.float32)
    inv_freq = theta ** (-jnp.arange(0, head_size // 2, dtype=jnp.float32) * 2.0 / head_size)
    angles = positions[:, None] * inv_freq[None, :]
    return (jnp.cos(angles)[:, None, :], jnp.sin(angles)[:, None, :])

def rotate(vector, cosine, sine_table):
    half_size = vector.shape[-1] // 2
    front_half = vector[..., :half_size]
    back_half = vector[..., half_size:]
    return jnp.concatenate([front_half * cosine - back_half * sine_table, front_half * sine_table + back_half * cosine], axis=-1)

def normed(vector, gain_vec):
    return vector * lax.rsqrt(lax.optimization_barrier(jnp.mean(vector * vector, axis=-1, keepdims=True)) + eps) * gain_vec

def matmul_high(left_side, right_side):
    return jnp.dot(left_side, right_side, precision=lax.Precision.HIGHEST)

def attend(q_rot, k_rot, v_rows):
    row_count = q_rot.shape[0]
    grouped = q_rot.reshape(row_count, KVH, QH // KVH, HEAD)
    scores = jnp.einsum('qgrd,kgd->grqk', grouped, k_rot, precision=lax.Precision.HIGHEST) * HEAD ** (-0.5)
    scores = low_back(scores)
    allowed = jnp.arange(row_count)[None, :] <= jnp.arange(row_count)[:, None]
    masked = jnp.where(allowed, scores, -1e+30)
    row_max = lax.optimization_barrier(jnp.max(masked, axis=-1, keepdims=True))
    expo = jnp.exp(masked - row_max)
    attn_probs = low(expo / lax.optimization_barrier(jnp.sum(expo, axis=-1, keepdims=True)))
    attn_mixed = jnp.einsum('grqk,kgd->qgrd', attn_probs, v_rows, precision=lax.Precision.HIGHEST)
    return attn_mixed.reshape(row_count, QH * HEAD)

def layer(layer_in, weights, cosine, sine_table):
    gain_one, w_query, w_key, w_value, w_out, gain_two, w_gate, w_up, w_down = weights
    row_count = layer_in.shape[0]
    xn_one = low(normed(layer_in, gain_one))
    q_all = low_back(matmul_high(xn_one, w_query)).reshape(row_count, QH, HEAD)
    k_all = low_back(matmul_high(xn_one, w_key)).reshape(row_count, KVH, HEAD)
    v_all = low(low_back(matmul_high(xn_one, w_value))).reshape(row_count, KVH, HEAD)
    q_rot = low(rotate(q_all, cosine, sine_table))
    k_rot = low(rotate(k_all, cosine, sine_table))
    attn_mixed = low(low_back(attend(q_rot, k_rot, v_all)))
    middle = layer_in + low_back(matmul_high(attn_mixed, w_out))
    xn_two = low(normed(middle, gain_two))
    gate_pre = low_back(matmul_high(xn_two, w_gate))
    up_pre = low_back(matmul_high(xn_two, w_up))
    hidden = low(jax.nn.silu(gate_pre) * up_pre)
    return middle + low_back(matmul_high(hidden, w_down))

def reference(tokens, cotangent, attn_gain, w_query, w_key, w_value, w_out, mlp_gain, w_gate, w_up, w_down):
    params = tuple((matrix.astype(jnp.float32) for matrix in (attn_gain, w_query, w_key, w_value, w_out, mlp_gain, w_gate, w_up, w_down)))
    inputs = tokens.astype(jnp.float32).reshape(N_DP, SEQ, D)
    upstream = cotangent.astype(jnp.float32).reshape(N_DP, SEQ, D)
    cosine, sine_table = rope_angles(0, SEQ, HEAD)

    def forward(weights, layer_in, probe):

        def one_sequence(sequence_pair):
            seq_rows, probe_rows = sequence_pair
            first_out = low(layer(seq_rows, tuple((matrix[0] for matrix in weights)), cosine, sine_table))
            second_in = low_back(first_out + probe_rows)
            return (first_out, layer(second_in, tuple((matrix[1] for matrix in weights)), cosine, sine_table))
        return lax.map(jax.checkpoint(one_sequence), (layer_in, probe))
    probe = jnp.zeros_like(inputs)
    section_outs, pull_back = jax.vjp(forward, params, inputs, probe)
    weight_grads, grad_first, grad_second = pull_back((jnp.zeros_like(section_outs[0]), upstream))
    activations = jnp.stack([section_outs[0], section_outs[1]]).reshape(2, TOKENS, D).astype(jnp.bfloat16)
    input_grads = jnp.stack([grad_first, grad_second]).reshape(2, TOKENS, D)
    return (activations, input_grads, weight_grads[0], weight_grads[1], weight_grads[2], weight_grads[3], weight_grads[4], weight_grads[5], weight_grads[6], weight_grads[7], weight_grads[8])
```

```python
import jax
import jax.numpy as jnp
from jax import lax
from jax.experimental import pallas as pl
from jax.experimental.pallas import tpu as pltpu
from jax.sharding import PartitionSpec as P

HEAD = 64
LANES = 128
EPS = 1e-05
THETA = 500000.0
GROUPS = 2
VMEM_BYTES = 56 * 1024 * 1024
f32 = jnp.float32
bf16 = jnp.bfloat16


def rope_tables(positions):
    inv_freq = THETA ** (-jnp.arange(0, HEAD // 2, dtype=f32) * 2.0 / HEAD)
    angles = positions.astype(f32)[:, None] * inv_freq[None, :]
    cosine, sine = jnp.cos(angles), jnp.sin(angles)
    return jnp.concatenate([cosine] * 4, axis=1), jnp.concatenate([-sine, sine] * 2, axis=1)


def normed(vector, gain):
    return vector * lax.rsqrt(jnp.mean(vector * vector, axis=-1, keepdims=True) + EPS) * gain


def gated_units(gate, up):
    return jax.nn.silu(gate) * up


def dot(a, b):
    return jnp.dot(a, b, preferred_element_type=f32)


def dot_nt(a, b):
    return lax.dot_general(a, b, (((1,), (1,)), ((), ())), preferred_element_type=f32)


def dot_tn(a, b):
    return lax.dot_general(a, b, (((0,), (0,)), ((), ())), preferred_element_type=f32)


def to_core(block):
    return lax.ppermute(block, "tensor", [(0, 1), (1, 0)])


def to_plane(block):
    return lax.ppermute(block, "pipe", [(0, 1), (1, 0)])


def to_dp(block, flip):
    return lax.ppermute(block, "dp", [(i, i ^ flip) for i in range(lax.axis_size("dp"))])


def to_diagonal(block):
    n = lax.axis_size("dp")
    route = [(p * n + i, (1 - p) * n + (i ^ 1)) for p in range(2) for i in range(n)]
    return lax.ppermute(block, ("pipe", "dp"), route)


def column_groups():
    column = lax.axis_size("dp") // 2
    size = column // GROUPS
    return [range(g * size, (g + 1) * size) for g in range(GROUPS)]


def gather_tokens(block):
    out = []
    for group in column_groups():
        column = jnp.concatenate([block if k == 0 else to_dp(block, 2 * k) for k in group], axis=0)
        out.append(
            jnp.concatenate(
                [column, to_dp(column, 1), to_plane(column), to_diagonal(column)], axis=0
            )
        )
    return out


def sum_tokens(partials):
    total = None
    for group, (kept, beside, across, diagonal) in zip(column_groups(), partials):
        rows = kept.shape[0] // len(group)
        column = (
            kept
            + to_dp(beside, 1).astype(f32)
            + to_plane(across).astype(f32)
            + to_diagonal(diagonal).astype(f32)
        )
        for place, k in enumerate(group):
            part = column[place * rows : (place + 1) * rows]
            if k:
                part = to_dp(part.astype(bf16), 2 * k).astype(f32)
            total = part if total is None else total + part
    return total


def gather_four(block):
    pair = jnp.concatenate([block, to_plane(block)], axis=0)
    return jnp.concatenate([pair, to_core(pair)], axis=0)


def sum_four(kept, sent):
    pair = kept + to_core(sent).astype(f32)
    own = pair.shape[0] // 2
    return pair[:own] + to_plane(pair[own:].astype(bf16)).astype(f32)


def swapped_halves(tile):
    lane = lax.broadcasted_iota(jnp.int32, tile.shape, 1)
    up = pltpu.roll(tile, LANES - HEAD // 2, 1)
    down = pltpu.roll(tile, HEAD // 2, 1)
    return jnp.where(lane % HEAD < HEAD // 2, up, down)


def head_variants(tile):
    lane = lax.broadcasted_iota(jnp.int32, tile.shape, 1)
    low = jnp.where(lane < HEAD, tile, 0.0)
    high = jnp.where(lane < HEAD, 0.0, tile)
    turned = (pltpu.roll(low, HEAD, 1), pltpu.roll(high, HEAD, 1))
    return ((low.astype(bf16), turned[0].astype(bf16)), (turned[1].astype(bf16), high.astype(bf16)))


def softmax_rows(scores):
    expo = jnp.exp(scores - jnp.max(scores, axis=-1, keepdims=True))
    return expo / jnp.sum(expo, axis=-1, keepdims=True)


def listed(refs, count):
    if len(refs[0].shape) == 3:
        return [refs[0].at[j] for j in range(count)]
    return refs[:count]


def attend_forward_kernel(count, cols, q_width, offset_ref, x_ref, cos_ref, sin_ref, mask_ref, *refs):
    blocks = listed(refs, count)
    keep_ref, send_ref, q_ref, kv_ref, mixed_ref, xn_own_ref, gain_ref, xn_ref, full_ref = refs[-9:]
    rows = x_ref.shape[0]
    kv_width = LANES
    qkv_width = q_width + 2 * kv_width
    starts = [pl.multiple_of(offset_ref[j], cols) for j in range(count)]
    if count == 1:
        gain_ref[...] = refs[1][...].astype(f32)
    else:
        for start, block in zip(starts, blocks):
            gain_rows = block[cols:, :].astype(f32)
            for i in range(2):
                gain_ref[i : i + 1, pl.ds(start, cols)] = gain_rows[:1, i * cols : (i + 1) * cols]
    xn_ref[...] = normed(x_ref[...].astype(f32), gain_ref[0:1, :]).astype(bf16)
    xn_own_ref[...] = xn_ref[: xn_own_ref.shape[0], :]
    qkv = None
    for start, block in zip(starts, blocks):
        part = dot(xn_ref[:, pl.ds(start, cols)], block[:cols, :qkv_width])
        qkv = part if qkv is None else qkv + part
    cosine, sine, mask = cos_ref[...], sin_ref[...], mask_ref[...]

    def turned(tile):
        return tile * cosine + swapped_halves(tile) * sine

    keys = turned(qkv[:, q_width : q_width + kv_width]).astype(bf16)
    values = qkv[:, q_width + kv_width :].astype(bf16)
    kv_ref[:, :kv_width] = keys
    kv_ref[:, kv_width:] = values
    key_variants = head_variants(keys.astype(f32))
    value_variants = head_variants(values.astype(f32))
    tiles = q_width // LANES
    for i in range(tiles):
        kv_head = i * 2 // tiles
        tile = slice(i * LANES, (i + 1) * LANES)
        q_tile = turned(qkv[:, tile]).astype(bf16)
        q_ref[:, tile] = q_tile
        mixed = None
        for side in range(2):
            scores = dot_nt(q_tile, key_variants[kv_head][side]) * HEAD ** (-0.5) + mask
            part = dot(softmax_rows(scores).astype(bf16), value_variants[kv_head][side])
            mixed = part if mixed is None else mixed + part
        mixed_ref[:, tile] = mixed.astype(bf16)
    mixed = mixed_ref[...]
    for start, block in zip(starts, blocks):
        full_ref[:, pl.ds(start, cols)] = dot_nt(mixed, block[:cols, qkv_width:])
    keep_ref[...] = full_ref[: rows // 2, :]
    send_ref[...] = full_ref[rows // 2 :, :].astype(bf16)


def attend_backward_kernel(
    count, cols, q_width, offset_ref, d_ref, q_ref, kv_ref, cos_ref, sin_ref, mask_ref, *refs
):
    blocks = listed(refs, count)
    keep_ref, send_ref, d_qkv_ref, full_ref = refs[-4:]
    rows = d_ref.shape[0]
    kv_width = LANES
    qkv_width = q_width + 2 * kv_width
    scale = HEAD ** (-0.5)
    starts = [pl.multiple_of(offset_ref[j], cols) for j in range(count)]
    d_mixed = None
    for start, block in zip(starts, blocks):
        part = dot(d_ref[:, pl.ds(start, cols)], block[:cols, qkv_width:])
        d_mixed = part if d_mixed is None else d_mixed + part
    d_mixed = d_mixed.astype(bf16)
    cosine, sine, mask = cos_ref[...], sin_ref[...], mask_ref[...]

    def turned_back(tile):
        return tile * cosine - swapped_halves(tile) * sine

    key_variants = head_variants(kv_ref[:, :kv_width].astype(f32))
    value_variants = head_variants(kv_ref[:, kv_width:].astype(f32))
    tiles = q_width // LANES
    d_keys = [[None, None], [None, None]]
    d_values = [[None, None], [None, None]]
    for i in range(tiles):
        kv_head = i * 2 // tiles
        tile = slice(i * LANES, (i + 1) * LANES)
        q_tile = q_ref[:, tile]
        d_tile = d_mixed[:, tile]
        dq = None
        for side in range(2):
            scores = dot_nt(q_tile, key_variants[kv_head][side]) * scale + mask
            probs = softmax_rows(scores)
            d_probs = dot_nt(d_tile, value_variants[kv_head][side])
            delta = jnp.sum(probs * d_probs, axis=-1, keepdims=True)
            d_scores = (probs * (d_probs - delta)).astype(bf16)
            part = dot(d_scores, key_variants[kv_head][side])
            dq = part if dq is None else dq + part
            for store, lhs, rhs in ((d_keys, d_scores, q_tile), (d_values, probs.astype(bf16), d_tile)):
                part = dot_tn(lhs, rhs)
                before = store[kv_head][side]
                store[kv_head][side] = part if before is None else before + part
        d_qkv_ref[:, tile] = turned_back(dq * scale).astype(bf16)
    lane = lax.broadcasted_iota(jnp.int32, (rows, LANES), 1)

    def merged(store):
        heads = []
        for kv_head in range(2):
            low, high = store[kv_head]
            heads.append((low, high))
        first = heads[0][0] + pltpu.roll(heads[0][1], HEAD, 1)
        second = pltpu.roll(heads[1][0], HEAD, 1) + heads[1][1]
        return jnp.where(lane < HEAD, first, second)

    d_qkv_ref[:, q_width : q_width + kv_width] = turned_back(merged(d_keys) * scale).astype(bf16)
    d_qkv_ref[:, q_width + kv_width :] = merged(d_values).astype(bf16)
    d_qkv = d_qkv_ref[...]
    for start, block in zip(starts, blocks):
        full_ref[:, pl.ds(start, cols)] = dot_nt(d_qkv, block[:cols, :qkv_width])
    keep_ref[...] = full_ref[: rows // 2, :]
    send_ref[...] = full_ref[rows // 2 :, :].astype(bf16)


SMEM = pl.BlockSpec(memory_space=pltpu.SMEM)
VMEM = pl.BlockSpec(memory_space=pltpu.VMEM)
ANYWHERE = pl.BlockSpec(memory_space=pl.ANY)


def call(kernel, out_shape, specs, operands, pins, flops, scratch=(), out_specs=None, grid=(), aliases=None):
    pins = list(pins)
    moved = sum(a.size * a.dtype.itemsize for a in list(operands) + list(out_shape))
    return pl.pallas_call(
        kernel,
        grid=grid,
        out_shape=tuple(out_shape),
        in_specs=list(specs) + [ANYWHERE] * len(pins),
        out_specs=tuple(out_specs or [VMEM] * len(out_shape)),
        scratch_shapes=list(scratch),
        input_output_aliases=aliases or {},
        compiler_params=pltpu.CompilerParams(vmem_limit_bytes=VMEM_BYTES),
        cost_estimate=pl.CostEstimate(flops=flops, bytes_accessed=moved, transcendentals=0),
    )(*operands, *pins)


def attend_forward(offsets, x, tables, blocks, q_width, cols, pins=()):
    rows, width = x.shape
    count = offsets.shape[0]
    out_shape = (
        jax.ShapeDtypeStruct((rows // 2, width), f32),
        jax.ShapeDtypeStruct((rows // 2, width), bf16),
        jax.ShapeDtypeStruct((rows, q_width), bf16),
        jax.ShapeDtypeStruct((rows, 2 * LANES), bf16),
        jax.ShapeDtypeStruct((rows, q_width), bf16),
        jax.ShapeDtypeStruct((rows // 4, width), bf16),
        jax.ShapeDtypeStruct((2, width), f32),
    )
    return call(
        lambda *refs: attend_forward_kernel(count, cols, q_width, *refs),
        out_shape,
        [SMEM] + [VMEM] * (4 + len(blocks)),
        (offsets, x, *tables, *blocks),
        pins,
        2 * rows * width * blocks[0].shape[-1],
        [pltpu.VMEM((rows, width), bf16), pltpu.VMEM((rows, width), f32)],
    )


def attend_backward(offsets, d_attn, q_rot, kv, tables, blocks, cols, pins=()):
    rows, width = d_attn.shape
    q_width = q_rot.shape[1]
    count = offsets.shape[0]
    out_shape = (
        jax.ShapeDtypeStruct((rows // 2, width), f32),
        jax.ShapeDtypeStruct((rows // 2, width), bf16),
        jax.ShapeDtypeStruct((rows, q_width + 2 * LANES), bf16),
    )
    return call(
        lambda *refs: attend_backward_kernel(count, cols, q_width, *refs),
        out_shape,
        [SMEM] + [VMEM] * (6 + len(blocks)),
        (offsets, d_attn, q_rot, kv, *tables, *blocks),
        pins,
        2 * rows * width * blocks[0].shape[-1],
        [pltpu.VMEM((rows, width), f32)],
    )


def weight_views(refs, packed):
    if packed:
        return [[[ref.at[j, i] for j in range(ref.shape[0])] for i in range(3)] for ref in refs[:2]]
    return [[[refs[3 * half + i]] for i in range(3)] for half in range(2)]


def sliced_dot(x_ref, blocks, contract):
    total, start = None, 0
    for block in blocks:
        cols = block.shape[0] if contract is dot else block.shape[1]
        part = contract(x_ref[:, start : start + cols], block[...])
        total = part if total is None else total + part
        start += cols
    return total


def store_parts(outs, start, value):
    rows = value.shape[0] // 4
    for i, out_ref in enumerate(outs):
        part = value[i * rows : (i + 1) * rows]
        out_ref[:, start : start + value.shape[1]] = part.astype(out_ref.dtype)


def mlp_forward_kernel(packed, x_ref, *refs):
    views = weight_views(refs, packed)
    gate_ref, up_ref, hidden_ref = refs[-7:-4]
    units = gate_ref.shape[1] // 2
    hiddens = []
    for half, (gate_w, up_w, _) in enumerate(views):
        gate, up = sliced_dot(x_ref, gate_w, dot), sliced_dot(x_ref, up_w, dot)
        hiddens.append((gate * jax.nn.sigmoid(gate) * up).astype(bf16))
        place = slice(half * units, (half + 1) * units)
        gate_ref[:, place] = gate
        up_ref[:, place] = up
        hidden_ref[:, place] = hiddens[-1]
    start = 0
    for first, second in zip(views[0][2], views[1][2]):
        store_parts(refs[-4:], start, dot(hiddens[0], first[...]) + dot(hiddens[1], second[...]))
        start += first.shape[1]


def mlp_down_kernel(packed, rows, offset_ref, *refs):
    hiddens = refs[:GROUPS]
    views = weight_views(refs[GROUPS:], packed)
    out_ref = refs[-1]
    place = 0
    for hidden_ref in hiddens:
        hidden = hidden_ref[...]
        units = hidden.shape[1] // 2
        count = hidden.shape[0] // rows
        starts = [pl.multiple_of(offset_ref[place + i], rows) for i in range(count)]
        place += count
        start = 0
        for first, second in zip(views[0][2], views[1][2]):
            part = dot(hidden[:, :units], first[...]) + dot(hidden[:, units:], second[...])
            part = part.astype(bf16)
            for i in range(count):
                out_ref[pl.ds(starts[i], rows), start : start + part.shape[1]] = part[
                    i * rows : (i + 1) * rows
                ]
            start += part.shape[1]


def mlp_backward_kernel(packed, again, d_ref, *refs):
    given = refs[: 1 if again else 2]
    views = weight_views(refs[len(given) :], packed)
    d_gate_ref, d_up_ref = refs[-6:-4]
    units = d_gate_ref.shape[1] // 2
    d_gates, d_ups = [], []
    for half, (gate_w, up_w, down_w) in enumerate(views):
        place = slice(half * units, (half + 1) * units)
        d_hidden = sliced_dot(d_ref, down_w, dot_nt)
        if again:
            gate, up = sliced_dot(given[0], gate_w, dot), sliced_dot(given[0], up_w, dot)
            refs[-7][:, place] = (gate * jax.nn.sigmoid(gate) * up).astype(bf16)
        else:
            gate, up = given[0][:, place], given[1][:, place]
        gated = jax.nn.sigmoid(gate)
        d_ups.append((d_hidden * gate * gated).astype(bf16))
        d_gates.append((d_hidden * up * gated * (1.0 + gate * (1.0 - gated))).astype(bf16))
        d_gate_ref[:, place] = d_gates[-1]
        d_up_ref[:, place] = d_ups[-1]
    start = 0
    for blocks in zip(*views[0][:2], *views[1][:2]):
        total = None
        for value, block in zip((d_gates[0], d_ups[0], d_gates[1], d_ups[1]), blocks):
            part = dot_nt(value, block[...])
            total = part if total is None else total + part
        store_parts(refs[-4:], start, total)
        start += total.shape[1]


def weight_specs(layer, mats):
    specs = []
    for m in mats:
        if len(m.shape) == 4:
            specs.append(pl.BlockSpec((m.shape[0] // 2,) + m.shape[1:], lambda i: (layer, 0, 0, 0)))
        else:
            specs.append(pl.BlockSpec((None,) + m.shape[1:], lambda i: (layer, 0, 0)))
    return specs


def part_shapes(rows, width):
    return [jax.ShapeDtypeStruct((rows // 4, width), f32)] + [
        jax.ShapeDtypeStruct((rows // 4, width), bf16)
    ] * 3


def mlp_forward(layer, tokens, mats, units, pins=()):
    rows, width = tokens.shape
    out_shape = [
        jax.ShapeDtypeStruct((rows, 2 * units), f32),
        jax.ShapeDtypeStruct((rows, 2 * units), f32),
        jax.ShapeDtypeStruct((rows, 2 * units), bf16),
    ] + part_shapes(rows, width)
    return call(
        lambda *refs: mlp_forward_kernel(len(mats) == 2, *refs),
        out_shape,
        [VMEM] + weight_specs(layer, mats),
        (tokens, *mats),
        pins,
        12 * rows * width * units,
        grid=(1,),
    )


def mlp_down(layer, offsets, hiddens, mats, width, pins=()):
    rows = sum(h.shape[0] for h in hiddens)
    own = rows // offsets.shape[0]
    return call(
        lambda *refs: mlp_down_kernel(len(mats) == 2, own, *refs),
        [jax.ShapeDtypeStruct((rows, width), bf16)],
        [SMEM] + [VMEM] * len(hiddens) + weight_specs(layer, mats),
        (offsets * own, *hiddens, *mats),
        pins,
        2 * rows * width * hiddens[0].shape[1],
        grid=(1,),
    )[0]


def mlp_backward(layer, d_tokens, given, mats, units, again, pins=()):
    rows, width = d_tokens.shape
    out_shape = [jax.ShapeDtypeStruct((rows, 2 * units), bf16)] * (3 if again else 2)
    out_shape += part_shapes(rows, width)
    return call(
        lambda *refs: mlp_backward_kernel(len(mats) == 2, again, *refs),
        out_shape,
        [VMEM] * (1 + len(given)) + weight_specs(layer, mats),
        (d_tokens, *given, *mats),
        pins,
        (20 if again else 12) * rows * width * units,
        grid=(1,),
    )


def unit_grads_kernel(groups, *refs):
    outs = refs[-2:]
    units = refs[2].shape[1] // 2
    for half, out_ref in enumerate(outs):
        place = slice(half * units, (half + 1) * units)
        totals = [None, None, None]
        for g in range(groups):
            x_ref, d_ref, d_gate_ref, d_up_ref, hidden_ref = refs[g * 5 : g * 5 + 5]
            x, d = x_ref[...], d_ref[...]
            parts = (
                dot_tn(x, d_gate_ref[:, place]),
                dot_tn(x, d_up_ref[:, place]),
                dot_tn(hidden_ref[:, place], d),
            )
            totals = [p if t is None else t + p for t, p in zip(totals, parts)]
        for i in range(3):
            out_ref[0, i] = totals[i].astype(bf16)


def unit_grads(n, inputs, pins=()):
    rows, width = inputs[0][0].shape
    units = inputs[0][2].shape[1] // 2
    cols = width // n
    if cols % LANES:
        made = []
        for place in (slice(0, units), slice(units, 2 * units)):
            totals = [0.0, 0.0, 0.0]
            for x, d, d_gate, d_up, hidden in inputs:
                totals[0] += dot_tn(x, d_gate[:, place]).reshape(n, cols, units)
                totals[1] += dot_tn(x, d_up[:, place]).reshape(n, cols, units)
                totals[2] += dot_tn(hidden[:, place], d).reshape(units, n, cols).transpose(1, 0, 2)
            made.append(jnp.stack(totals, axis=1).astype(bf16))
        return made
    specs, operands = [], []
    for group in inputs:
        for place, array in enumerate(group):
            operands.append(array)
            if place < 2:
                specs.append(pl.BlockSpec((rows, cols), lambda j: (0, j)))
            else:
                specs.append(pl.BlockSpec(array.shape, lambda j: (0, 0)))
    return call(
        lambda *refs: unit_grads_kernel(len(inputs), *refs),
        [jax.ShapeDtypeStruct((n, 3, cols, units), bf16)] * 2,
        specs,
        operands,
        pins,
        12 * len(inputs) * rows * width * units,
        out_specs=[pl.BlockSpec((1, 3, cols, units), lambda j: (j, 0, 0, 0))] * 2,
        grid=(n,),
    )


def add_kernel(kept_ref, got_ref, *refs):
    refs[-1][...] = (kept_ref[...].astype(f32) + got_ref[...].astype(f32)).astype(bf16)


def core_sum(layer, kept, got, into, pins=()):
    n = kept.shape[0]
    if kept.shape[3] % LANES:
        made = (kept.astype(f32) + got.astype(f32)).astype(bf16)
        return made if into is None else jnp.concatenate([made, into], axis=0)
    block = (n // 2,) + kept.shape[1:]
    return call(
        add_kernel,
        [jax.ShapeDtypeStruct((2 * n,) + kept.shape[1:], bf16)],
        [pl.BlockSpec(block, lambda j: (j, 0, 0, 0))] * 2,
        (kept, got),
        ([] if into is None else [into]) + list(pins),
        0,
        out_specs=[pl.BlockSpec(block, lambda j: (2 * layer + j, 0, 0, 0))],
        grid=(2,),
        aliases={} if into is None else {2: 0},
    )[0]


def pack_kernel(gate_ref, up_ref, down_ref, *refs):
    out_ref = refs[-1]
    _, _, cols, units = out_ref.shape
    for i in range(out_ref.shape[0]):
        place = slice(i * units, (i + 1) * units)
        out_ref[i, 0] = gate_ref[:, place]
        out_ref[i, 1] = up_ref[:, place]
        out_ref[i, 2] = down_ref[place, :]


def unpack_kernel(in_ref, *refs):
    gate_ref, up_ref, down_ref = refs[-3:]
    _, _, cols, units = in_ref.shape
    for i in range(in_ref.shape[0]):
        place = slice(i * units, (i + 1) * units)
        gate_ref[:, place] = in_ref[i, 0].astype(f32)
        up_ref[:, place] = in_ref[i, 1].astype(f32)
        down_ref[place, :] = in_ref[i, 2].astype(f32)


def packing_specs(cols, units, steps):
    rows = pl.BlockSpec((cols, steps * units), lambda i: (0, i))
    columns = pl.BlockSpec((steps * units, cols), lambda i: (i, 0))
    packed = pl.BlockSpec((steps, 3, cols, units), lambda i: (i, 0, 0, 0))
    return [rows, rows, columns], packed


def packed_units(gate, up, down, pieces, pins):
    cols, units = gate.shape[0], gate.shape[1] // pieces
    specs, packed = packing_specs(cols, units, 4)
    return call(
        pack_kernel,
        [jax.ShapeDtypeStruct((pieces, 3, cols, units), gate.dtype)],
        specs,
        (gate, up, down),
        pins,
        0,
        out_specs=[packed],
        grid=(pieces // 4,),
    )[0]


def unpacked_units(packed_array, pins):
    pieces, _, cols, units = packed_array.shape
    specs, packed = packing_specs(cols, units, 4)
    return call(
        unpack_kernel,
        [
            jax.ShapeDtypeStruct((cols, pieces * units), f32),
            jax.ShapeDtypeStruct((cols, pieces * units), f32),
            jax.ShapeDtypeStruct((pieces * units, cols), f32),
        ],
        [packed],
        (packed_array,),
        pins,
        0,
        out_specs=specs,
        grid=(pieces // 4,),
    )


def on_device(
    tokens, cotangent, attn_gain, w_query, w_key, w_value, w_out, mlp_gain, w_gate, w_up, w_down
):
    plane = lax.axis_index("pipe")
    core = lax.axis_index("tensor")
    place = lax.axis_index("dp")
    n = lax.axis_size("dp")
    first = plane == 0
    seq_len, width = tokens.shape
    own_cols = width // n
    own = seq_len // 4
    q_width = w_query.shape[2] // 2
    kv_width = w_key.shape[2] // 2
    starts = [
        (2 * c + p) * own
        for c, p in ((core, plane), (core, 1 - plane), (1 - core, plane), (1 - core, 1 - plane))
    ]

    def own_rows(rows):
        return lax.dynamic_slice_in_dim(rows, starts[0], own, 0)

    def relative(rows):
        return jnp.concatenate(
            [lax.dynamic_slice_in_dim(rows, start, own, 0) for start in starts], axis=0
        )

    def natural(rows):
        out = jnp.zeros_like(rows)
        for i, start in enumerate(starts):
            out = lax.dynamic_update_slice_in_dim(out, rows[i * own : (i + 1) * own], start, 0)
        return out

    def halves(matrix, axis):
        return jnp.split(matrix, 2, axis=axis)

    units = w_gate.shape[2] // (2 * n)
    by_blocks = own_cols % LANES == 0 and units == own_cols and n == 8
    block_cols = own_cols if by_blocks else width
    gains = jnp.concatenate([attn_gain, mlp_gain], axis=0)
    packed = [
        jnp.concatenate([q, k, v, o.T], axis=1)
        for q, k, v, o in zip(
            halves(w_query[0], 1), halves(w_key[0], 1), halves(w_value[0], 1), halves(w_out[0], 0)
        )
    ]
    if by_blocks:
        row = jnp.pad(gains.reshape(1, -1), ((0, 15), (0, packed[0].shape[1] - 2 * own_cols)))
        packed = [jnp.concatenate([part, row], axis=0) for part in packed]
    got = to_plane(jnp.where(first, packed[1], packed[0]))
    local = [jnp.where(first, packed[0], got), jnp.where(first, got, packed[1])]
    own_cot = own_rows(cotangent)
    cot_all = gather_tokens(own_cot)
    both = ("pipe", "dp")

    if by_blocks:
        attn_blocks = [[lax.all_gather(block, "dp", axis=0)] for block in local]
        offsets = jnp.arange(n, dtype=jnp.int32) * own_cols
        packed_weights = packed_units(w_gate[0], w_up[0], w_down[0], 2 * n, [got] + cot_all)
        mats = [lax.all_to_all(packed_weights, both, 0, 0, tiled=True)]
    else:
        other_gains = to_plane(gains)
        local_gains = [jnp.where(first, gains, other_gains), jnp.where(first, other_gains, gains)]
        attn_blocks = [
            [
                lax.all_gather(block, "dp", axis=0, tiled=True),
                lax.all_gather(gain, "dp", axis=1, tiled=True),
            ]
            for block, gain in zip(local, local_gains)
        ]
        offsets = jnp.zeros((1,), jnp.int32)
        down_both = lax.all_to_all(w_down[0], both, 0, 0, tiled=True).reshape(2, n, units, own_cols)
        mats = [
            lax.all_to_all(w_gate[0], both, 1, 0, tiled=True).reshape(2, width, units),
            lax.all_to_all(w_up[0], both, 1, 0, tiled=True).reshape(2, width, units),
            down_both.transpose(0, 2, 1, 3).reshape(2, units, width),
        ]
    mats = mats + [to_core(m) for m in mats]

    positions = jnp.concatenate([start + jnp.arange(own, dtype=jnp.int32) for start in starts])
    causal = positions[None, :] <= positions[:, None]
    tables = rope_tables(positions) + (jnp.where(causal, 0.0, -1e30).astype(f32),)

    def attention(layer, layer_in):
        keep, send, q_rot, kv, mixed, xn_own, gains = attend_forward(
            offsets, layer_in, tables, attn_blocks[layer], q_width, block_cols
        )
        middle = layer_in[:own].astype(f32) + sum_four(keep, send)
        xn_two = gather_tokens(normed(middle, gains[1:2]).astype(bf16))
        return xn_two, middle, (gains, xn_own, q_rot, kv, mixed)

    def d_attention(layer, d_middle, layer_in, kept, pins=()):
        gains, xn_own, q_rot, kv, mixed = kept
        keep, send, d_qkv = attend_backward(
            offsets,
            gather_four(d_middle.astype(bf16)),
            q_rot,
            kv,
            tables,
            attn_blocks[layer],
            block_cols,
            pins,
        )
        d_xn_one = sum_four(keep, send)
        _, norm_pull = jax.vjp(normed, layer_in[:own].astype(f32), gains[0:1])
        d_in_norm, d_gain_one = norm_pull(d_xn_one)
        return d_middle + d_in_norm, d_qkv, d_gain_one

    def d_norm(upstream, d_xn_two, middle, gains):
        _, norm_pull = jax.vjp(normed, middle, gains[1:2])
        d_mid_norm, d_gain_two = norm_pull(d_xn_two)
        return upstream.astype(f32) + d_mid_norm, d_gain_two

    def grad_inputs(xs, d_tokens, d_units, hiddens):
        return [
            (x, d, du[0], du[1], h) for x, d, du, h in zip(xs, d_tokens, d_units, hiddens)
        ]

    def dp_all(block, axis):
        return lax.all_gather(block, "dp", axis=axis, tiled=True)

    in_first = relative(tokens)
    xn_first, middle_first, kept_first = attention(0, in_first)
    units_first = [mlp_forward(0, x, mats, units) for x in xn_first]
    first_out = (middle_first + sum_tokens([r[3:] for r in units_first])).astype(bf16)
    in_second = gather_four(first_out)
    xn_second, middle_second, kept_second = attention(1, in_second)
    units_second = [
        mlp_backward(1, d, [x], mats, units, True) for d, x in zip(cot_all, xn_second)
    ]
    hidden_second = [r[0] for r in units_second]
    d_units_second = [r[1:] for r in units_second]
    d_middle_second, d_mlp_gain_second = d_norm(
        own_cot, sum_tokens([d[2:] for d in d_units_second]), middle_second, kept_second[0]
    )
    mixed_all = dp_all(jnp.stack([kept_first[4], kept_second[4]]), 1)
    d_second, d_qkv_second, d_attn_gain_second = d_attention(
        1, d_middle_second, in_second, kept_second
    )
    d_second = d_second.astype(bf16)
    d_qkv_second_all = dp_all(d_qkv_second, 0)
    d_all = gather_tokens(d_second)
    made, sent = unit_grads(
        n, grad_inputs(xn_second, cot_all, d_units_second, hidden_second), [d_second]
    )
    packed_grads = core_sum(1, made, to_core(sent), None)
    owners = jnp.stack(
        [
            (place ^ (2 * k + j % 2)) * 2 + (plane ^ (j // 2))
            for group in column_groups()
            for j in range(4)
            for k in group
        ]
    )
    partial = mlp_down(1, owners, hidden_second, mats, width, [d_middle_second])
    partial = lax.psum_scatter(partial, ("dp", "pipe"), scatter_dimension=0, tiled=True)
    second_out = (middle_second + partial.astype(f32)).astype(bf16)
    d_units_first = [
        mlp_backward(0, d, r[:2], mats, units, False, [mixed_all])
        for d, r in zip(d_all, units_first)
    ]
    made, sent = unit_grads(
        n, grad_inputs(xn_first, d_all, d_units_first, [r[2] for r in units_first])
    )
    d_middle_first, d_mlp_gain_first = d_norm(
        d_second, sum_tokens([d[2:] for d in d_units_first]), middle_first, kept_first[0]
    )
    packed_grads = core_sum(0, made, to_core(sent), packed_grads, [d_middle_first])
    d_first, d_qkv_first, d_attn_gain_first = d_attention(
        0, d_middle_first, in_first, kept_first, [d_qkv_second_all]
    )
    gain_rows = jnp.concatenate(
        [d_attn_gain_first, d_mlp_gain_first, d_attn_gain_second, d_mlp_gain_second]
    ).astype(bf16)
    pad_rows = -(-gain_rows.size // (16 * d_qkv_first.shape[1])) * 16
    gain_rows = jnp.pad(
        gain_rows.reshape(-1), (0, pad_rows * d_qkv_first.shape[1] - gain_rows.size)
    ).reshape(pad_rows, -1)
    gathered = lax.all_gather(jnp.concatenate([d_qkv_first, gain_rows]), "dp", axis=0)
    d_qkv_first_all = gathered[:, :seq_len].reshape(n * seq_len, -1)
    gain_sums = jnp.sum(gathered[:, seq_len:].astype(f32), axis=0).reshape(-1)
    gain_sums = gain_sums[: 4 * width].reshape(4, width)
    gain_sums = gain_sums + to_core(gain_sums)
    gain_sums = gain_sums + to_plane(gain_sums)

    columns = jnp.stack(
        [kept_first[1], d_middle_first.astype(bf16), kept_second[1], d_middle_second.astype(bf16)]
    )
    columns = lax.all_to_all(columns.reshape(4 * own, n, own_cols), "dp", 1, 0)
    columns = gather_four(columns.reshape(1, n, 4, own, own_cols))
    columns = columns.transpose(2, 1, 0, 3, 4).reshape(4, n * seq_len, own_cols)

    def attention_grads(layer, d_qkv_all):
        return jnp.concatenate(
            [
                dot_tn(columns[2 * layer], d_qkv_all),
                dot_tn(columns[2 * layer + 1], mixed_all[layer]),
            ],
            axis=1,
        ).astype(bf16)

    small_first = attention_grads(0, d_qkv_first_all)
    small_second = attention_grads(1, d_qkv_second_all)
    small_own = jnp.where(first, small_first, small_second)
    small_got = to_plane(jnp.where(first, small_second, small_first))
    small = [
        jnp.where(first, small_own, small_got).astype(f32),
        jnp.where(first, small_got, small_own).astype(f32),
    ]

    def joined(start, size):
        return jnp.concatenate([part[:, start : start + size] for part in small], axis=1)

    grad_query = joined(0, q_width)
    grad_key = joined(q_width, kv_width)
    grad_value = joined(q_width + kv_width, kv_width)
    grad_out = joined(q_width + 2 * kv_width, q_width).T
    packed_grads = lax.all_to_all(packed_grads, both, 0, 0, tiled=True)
    if by_blocks:
        grad_gate, grad_up, grad_down = unpacked_units(packed_grads, [small_got, gain_sums, second_out])
    else:
        parts = [packed_grads[:, i].astype(f32) for i in range(3)]
        grad_gate, grad_up = [part.transpose(1, 0, 2).reshape(own_cols, -1) for part in parts[:2]]
        grad_down = parts[2].reshape(-1, own_cols)
    gain_sums = jnp.where(first, gain_sums[:2], gain_sums[2:])
    gain_grads = lax.dynamic_slice_in_dim(gain_sums, place * own_cols, own_cols, 1)

    activations = natural(jnp.where(first, in_second, gather_four(second_out)))
    input_grads = natural(
        jnp.where(first, gather_four(d_first), gather_four(d_second).astype(f32))
    )
    return (
        activations[None],
        input_grads[None],
        gain_grads[0][None],
        grad_query[None],
        grad_key[None],
        grad_value[None],
        grad_out[None],
        gain_grads[1][None],
        grad_gate[None],
        grad_up[None],
        grad_down[None],
    )


def solution(mesh):
    token_spec = P("dp", None)
    gain_spec = P("pipe", "dp")
    row_spec = P("pipe", "dp", "tensor")
    col_spec = P("pipe", "tensor", "dp")
    in_specs = (
        token_spec,
        token_spec,
        gain_spec,
        row_spec,
        row_spec,
        row_spec,
        col_spec,
        gain_spec,
        row_spec,
        row_spec,
        col_spec,
    )
    out_specs = (
        P("pipe", "dp", None),
        P("pipe", "dp", None),
        gain_spec,
        row_spec,
        row_spec,
        row_spec,
        col_spec,
        gain_spec,
        row_spec,
        row_spec,
        col_spec,
    )
    return jax.shard_map(
        on_device, mesh=mesh, in_specs=in_specs, out_specs=out_specs, check_vma=False
    )
```

```python
import jax
import jax.numpy as jnp
from jax import lax
from jax.experimental import pallas as pl
from jax.experimental.pallas import tpu as pltpu
from jax.sharding import PartitionSpec as P

HEAD = 64
LANES = 128
EPS = 1e-05
THETA = 500000.0
GROUPS = 2
VMEM_BYTES = 56 * 1024 * 1024
f32 = jnp.float32
bf16 = jnp.bfloat16


def rope_tables(positions):
    inv_freq = THETA ** (-jnp.arange(0, HEAD // 2, dtype=f32) * 2.0 / HEAD)
    angles = positions.astype(f32)[:, None] * inv_freq[None, :]
    cosine, sine = jnp.cos(angles), jnp.sin(angles)
    return jnp.concatenate([cosine] * 4, axis=1), jnp.concatenate([-sine, sine] * 2, axis=1)


def normed(vector, gain):
    return vector * lax.rsqrt(jnp.mean(vector * vector, axis=-1, keepdims=True) + EPS) * gain


def gated_units(gate, up):
    return jax.nn.silu(gate) * up


def dot(a, b):
    return jnp.dot(a, b, preferred_element_type=f32)


def dot_nt(a, b):
    return lax.dot_general(a, b, (((1,), (1,)), ((), ())), preferred_element_type=f32)


def dot_tn(a, b):
    return lax.dot_general(a, b, (((0,), (0,)), ((), ())), preferred_element_type=f32)


def to_core(block):
    return lax.ppermute(block, "tensor", [(0, 1), (1, 0)])


def to_plane(block):
    return lax.ppermute(block, "pipe", [(0, 1), (1, 0)])


def to_dp(block, flip):
    return lax.ppermute(block, "dp", [(i, i ^ flip) for i in range(lax.axis_size("dp"))])


def to_diagonal(block):
    n = lax.axis_size("dp")
    route = [(p * n + i, (1 - p) * n + (i ^ 1)) for p in range(2) for i in range(n)]
    return lax.ppermute(block, ("pipe", "dp"), route)


def column_groups():
    column = lax.axis_size("dp") // 2
    size = column // GROUPS
    return [range(g * size, (g + 1) * size) for g in range(GROUPS)]


def gather_tokens(block):
    out = []
    for group in column_groups():
        column = jnp.concatenate([block if k == 0 else to_dp(block, 2 * k) for k in group], axis=0)
        out.append(
            jnp.concatenate(
                [column, to_dp(column, 1), to_plane(column), to_diagonal(column)], axis=0
            )
        )
    return out


def sum_tokens(partials):
    total = None
    for group, (kept, beside, across, diagonal) in zip(column_groups(), partials):
        rows = kept.shape[0] // len(group)
        column = (
            kept
            + to_dp(beside, 1).astype(f32)
            + to_plane(across).astype(f32)
            + to_diagonal(diagonal).astype(f32)
        )
        for place, k in enumerate(group):
            part = column[place * rows : (place + 1) * rows]
            if k:
                part = to_dp(part.astype(bf16), 2 * k).astype(f32)
            total = part if total is None else total + part
    return total


def gather_four(block):
    pair = jnp.concatenate([block, to_plane(block)], axis=0)
    return jnp.concatenate([pair, to_core(pair)], axis=0)


def sum_four(kept, sent):
    pair = kept + to_core(sent).astype(f32)
    own = pair.shape[0] // 2
    return pair[:own] + to_plane(pair[own:].astype(bf16)).astype(f32)


def swapped_halves(tile):
    lane = lax.broadcasted_iota(jnp.int32, tile.shape, 1)
    up = pltpu.roll(tile, LANES - HEAD // 2, 1)
    down = pltpu.roll(tile, HEAD // 2, 1)
    return jnp.where(lane % HEAD < HEAD // 2, up, down)


def head_variants(tile):
    lane = lax.broadcasted_iota(jnp.int32, tile.shape, 1)
    low = jnp.where(lane < HEAD, tile, 0.0)
    high = jnp.where(lane < HEAD, 0.0, tile)
    turned = (pltpu.roll(low, HEAD, 1), pltpu.roll(high, HEAD, 1))
    return ((low.astype(bf16), turned[0].astype(bf16)), (turned[1].astype(bf16), high.astype(bf16)))


def softmax_rows(scores):
    expo = jnp.exp(scores - jnp.max(scores, axis=-1, keepdims=True))
    return expo / jnp.sum(expo, axis=-1, keepdims=True)


def listed(refs, count):
    if len(refs[0].shape) == 3:
        return [refs[0].at[j] for j in range(count)]
    return refs[:count]


def attend_forward_kernel(count, cols, q_width, offset_ref, x_ref, cos_ref, sin_ref, mask_ref, *refs):
    blocks = listed(refs, count)
    keep_ref, send_ref, q_ref, kv_ref, mixed_ref, xn_own_ref, gain_ref, xn_ref, full_ref = refs[-9:]
    rows = x_ref.shape[0]
    kv_width = LANES
    qkv_width = q_width + 2 * kv_width
    starts = [pl.multiple_of(offset_ref[j], cols) for j in range(count)]
    if count == 1:
        gain_ref[...] = refs[1][...].astype(f32)
    else:
        for start, block in zip(starts, blocks):
            gain_rows = block[cols:, :].astype(f32)
            for i in range(2):
                gain_ref[i : i + 1, pl.ds(start, cols)] = gain_rows[:1, i * cols : (i + 1) * cols]
    xn_ref[...] = normed(x_ref[...].astype(f32), gain_ref[0:1, :]).astype(bf16)
    xn_own_ref[...] = xn_ref[: xn_own_ref.shape[0], :]
    qkv = None
    for start, block in zip(starts, blocks):
        part = dot(xn_ref[:, pl.ds(start, cols)], block[:cols, :qkv_width])
        qkv = part if qkv is None else qkv + part
    cosine, sine, mask = cos_ref[...], sin_ref[...], mask_ref[...]

    def turned(tile):
        return tile * cosine + swapped_halves(tile) * sine

    keys = turned(qkv[:, q_width : q_width + kv_width]).astype(bf16)
    values = qkv[:, q_width + kv_width :].astype(bf16)
    kv_ref[:, :kv_width] = keys
    kv_ref[:, kv_width:] = values
    key_variants = head_variants(keys.astype(f32))
    value_variants = head_variants(values.astype(f32))
    tiles = q_width // LANES
    for i in range(tiles):
        kv_head = i * 2 // tiles
        tile = slice(i * LANES, (i + 1) * LANES)
        q_tile = turned(qkv[:, tile]).astype(bf16)
        q_ref[:, tile] = q_tile
        mixed = None
        for side in range(2):
            scores = dot_nt(q_tile, key_variants[kv_head][side]) * HEAD ** (-0.5) + mask
            part = dot(softmax_rows(scores).astype(bf16), value_variants[kv_head][side])
            mixed = part if mixed is None else mixed + part
        mixed_ref[:, tile] = mixed.astype(bf16)
    mixed = mixed_ref[...]
    for start, block in zip(starts, blocks):
        full_ref[:, pl.ds(start, cols)] = dot_nt(mixed, block[:cols, qkv_width:])
    keep_ref[...] = full_ref[: rows // 2, :]
    send_ref[...] = full_ref[rows // 2 :, :].astype(bf16)


def attend_backward_kernel(
    count, cols, q_width, offset_ref, d_ref, q_ref, kv_ref, cos_ref, sin_ref, mask_ref, *refs
):
    blocks = listed(refs, count)
    keep_ref, send_ref, d_qkv_ref, full_ref = refs[-4:]
    rows = d_ref.shape[0]
    kv_width = LANES
    qkv_width = q_width + 2 * kv_width
    scale = HEAD ** (-0.5)
    starts = [pl.multiple_of(offset_ref[j], cols) for j in range(count)]
    d_mixed = None
    for start, block in zip(starts, blocks):
        part = dot(d_ref[:, pl.ds(start, cols)], block[:cols, qkv_width:])
        d_mixed = part if d_mixed is None else d_mixed + part
    d_mixed = d_mixed.astype(bf16)
    cosine, sine, mask = cos_ref[...], sin_ref[...], mask_ref[...]

    def turned_back(tile):
        return tile * cosine - swapped_halves(tile) * sine

    key_variants = head_variants(kv_ref[:, :kv_width].astype(f32))
    value_variants = head_variants(kv_ref[:, kv_width:].astype(f32))
    tiles = q_width // LANES
    d_keys = [[None, None], [None, None]]
    d_values = [[None, None], [None, None]]
    for i in range(tiles):
        kv_head = i * 2 // tiles
        tile = slice(i * LANES, (i + 1) * LANES)
        q_tile = q_ref[:, tile]
        d_tile = d_mixed[:, tile]
        dq = None
        for side in range(2):
            scores = dot_nt(q_tile, key_variants[kv_head][side]) * scale + mask
            probs = softmax_rows(scores)
            d_probs = dot_nt(d_tile, value_variants[kv_head][side])
            delta = jnp.sum(probs * d_probs, axis=-1, keepdims=True)
            d_scores = (probs * (d_probs - delta)).astype(bf16)
            part = dot(d_scores, key_variants[kv_head][side])
            dq = part if dq is None else dq + part
            for store, lhs, rhs in ((d_keys, d_scores, q_tile), (d_values, probs.astype(bf16), d_tile)):
                part = dot_tn(lhs, rhs)
                before = store[kv_head][side]
                store[kv_head][side] = part if before is None else before + part
        d_qkv_ref[:, tile] = turned_back(dq * scale).astype(bf16)
    lane = lax.broadcasted_iota(jnp.int32, (rows, LANES), 1)

    def merged(store):
        heads = []
        for kv_head in range(2):
            low, high = store[kv_head]
            heads.append((low, high))
        first = heads[0][0] + pltpu.roll(heads[0][1], HEAD, 1)
        second = pltpu.roll(heads[1][0], HEAD, 1) + heads[1][1]
        return jnp.where(lane < HEAD, first, second)

    d_qkv_ref[:, q_width : q_width + kv_width] = turned_back(merged(d_keys) * scale).astype(bf16)
    d_qkv_ref[:, q_width + kv_width :] = merged(d_values).astype(bf16)
    d_qkv = d_qkv_ref[...]
    for start, block in zip(starts, blocks):
        full_ref[:, pl.ds(start, cols)] = dot_nt(d_qkv, block[:cols, :qkv_width])
    keep_ref[...] = full_ref[: rows // 2, :]
    send_ref[...] = full_ref[rows // 2 :, :].astype(bf16)


SMEM = pl.BlockSpec(memory_space=pltpu.SMEM)
VMEM = pl.BlockSpec(memory_space=pltpu.VMEM)
ANYWHERE = pl.BlockSpec(memory_space=pl.ANY)


def call(kernel, out_shape, specs, operands, pins, flops, scratch=(), out_specs=None, grid=(), aliases=None):
    pins = list(pins)
    moved = sum(a.size * a.dtype.itemsize for a in list(operands) + list(out_shape))
    return pl.pallas_call(
        kernel,
        grid=grid,
        out_shape=tuple(out_shape),
        in_specs=list(specs) + [ANYWHERE] * len(pins),
        out_specs=tuple(out_specs or [VMEM] * len(out_shape)),
        scratch_shapes=list(scratch),
        input_output_aliases=aliases or {},
        compiler_params=pltpu.CompilerParams(vmem_limit_bytes=VMEM_BYTES),
        cost_estimate=pl.CostEstimate(flops=flops, bytes_accessed=moved, transcendentals=0),
    )(*operands, *pins)


def after(array, pins):
    return call(
        lambda *refs: None,
        [jax.ShapeDtypeStruct(array.shape, array.dtype)],
        [ANYWHERE],
        (array,),
        pins,
        0,
        out_specs=[ANYWHERE],
        aliases={0: 0},
    )[0]


def attend_forward(offsets, x, tables, blocks, q_width, cols, pins=()):
    rows, width = x.shape
    count = offsets.shape[0]
    out_shape = (
        jax.ShapeDtypeStruct((rows // 2, width), f32),
        jax.ShapeDtypeStruct((rows // 2, width), bf16),
        jax.ShapeDtypeStruct((rows, q_width), bf16),
        jax.ShapeDtypeStruct((rows, 2 * LANES), bf16),
        jax.ShapeDtypeStruct((rows, q_width), bf16),
        jax.ShapeDtypeStruct((rows // 4, width), bf16),
        jax.ShapeDtypeStruct((2, width), f32),
    )
    return call(
        lambda *refs: attend_forward_kernel(count, cols, q_width, *refs),
        out_shape,
        [SMEM] + [VMEM] * (4 + len(blocks)),
        (offsets, x, *tables, *blocks),
        pins,
        2 * rows * width * blocks[0].shape[-1],
        [pltpu.VMEM((rows, width), bf16), pltpu.VMEM((rows, width), f32)],
    )


def attend_backward(offsets, d_attn, q_rot, kv, tables, blocks, cols, pins=()):
    rows, width = d_attn.shape
    q_width = q_rot.shape[1]
    count = offsets.shape[0]
    out_shape = (
        jax.ShapeDtypeStruct((rows // 2, width), f32),
        jax.ShapeDtypeStruct((rows // 2, width), bf16),
        jax.ShapeDtypeStruct((rows, q_width + 2 * LANES), bf16),
    )
    return call(
        lambda *refs: attend_backward_kernel(count, cols, q_width, *refs),
        out_shape,
        [SMEM] + [VMEM] * (6 + len(blocks)),
        (offsets, d_attn, q_rot, kv, *tables, *blocks),
        pins,
        2 * rows * width * blocks[0].shape[-1],
        [pltpu.VMEM((rows, width), f32)],
    )


def weight_views(refs, packed):
    if packed:
        return [[[ref.at[j, i] for j in range(ref.shape[0])] for i in range(3)] for ref in refs[:2]]
    return [[[refs[3 * half + i]] for i in range(3)] for half in range(2)]


def sliced_dot(x_ref, blocks, contract):
    total, start = None, 0
    for block in blocks:
        cols = block.shape[0] if contract is dot else block.shape[1]
        part = contract(x_ref[:, start : start + cols], block[...])
        total = part if total is None else total + part
        start += cols
    return total


def store_parts(outs, start, value):
    rows = value.shape[0] // 4
    for i, out_ref in enumerate(outs):
        part = value[i * rows : (i + 1) * rows]
        out_ref[:, start : start + value.shape[1]] = part.astype(out_ref.dtype)


def mlp_forward_kernel(packed, x_ref, *refs):
    views = weight_views(refs, packed)
    gate_ref, up_ref, hidden_ref = refs[-7:-4]
    units = gate_ref.shape[1] // 2
    hiddens = []
    for half, (gate_w, up_w, _) in enumerate(views):
        gate, up = sliced_dot(x_ref, gate_w, dot), sliced_dot(x_ref, up_w, dot)
        hiddens.append((gate * jax.nn.sigmoid(gate) * up).astype(bf16))
        place = slice(half * units, (half + 1) * units)
        gate_ref[:, place] = gate
        up_ref[:, place] = up
        hidden_ref[:, place] = hiddens[-1]
    start = 0
    for first, second in zip(views[0][2], views[1][2]):
        store_parts(refs[-4:], start, dot(hiddens[0], first[...]) + dot(hiddens[1], second[...]))
        start += first.shape[1]


def mlp_down_kernel(packed, rows, offset_ref, *refs):
    hiddens = refs[:GROUPS]
    views = weight_views(refs[GROUPS:], packed)
    out_ref = refs[-1]
    place = 0
    for hidden_ref in hiddens:
        hidden = hidden_ref[...]
        units = hidden.shape[1] // 2
        count = hidden.shape[0] // rows
        starts = [pl.multiple_of(offset_ref[place + i], rows) for i in range(count)]
        place += count
        start = 0
        for first, second in zip(views[0][2], views[1][2]):
            part = dot(hidden[:, :units], first[...]) + dot(hidden[:, units:], second[...])
            part = part.astype(bf16)
            for i in range(count):
                out_ref[pl.ds(starts[i], rows), start : start + part.shape[1]] = part[
                    i * rows : (i + 1) * rows
                ]
            start += part.shape[1]


def d_mlp_core(views, d_ref, given, units, outs, hidden_ref):
    d_gate_ref, d_up_ref = outs[:2]
    d_gates, d_ups = [], []
    for half, (gate_w, up_w, down_w) in enumerate(views):
        place = slice(half * units, (half + 1) * units)
        d_hidden = sliced_dot(d_ref, down_w, dot_nt)
        if hidden_ref is not None:
            gate, up = sliced_dot(given[0], gate_w, dot), sliced_dot(given[0], up_w, dot)
            hidden_ref[:, place] = (gate * jax.nn.sigmoid(gate) * up).astype(bf16)
        else:
            gate, up = given[0][:, place], given[1][:, place]
        gated = jax.nn.sigmoid(gate)
        d_ups.append((d_hidden * gate * gated).astype(bf16))
        d_gates.append((d_hidden * up * gated * (1.0 + gate * (1.0 - gated))).astype(bf16))
        d_gate_ref[:, place] = d_gates[-1]
        d_up_ref[:, place] = d_ups[-1]
    start = 0
    for blocks in zip(*views[0][:2], *views[1][:2]):
        total = None
        for value, block in zip((d_gates[0], d_ups[0], d_gates[1], d_ups[1]), blocks):
            part = dot_nt(value, block[...])
            total = part if total is None else total + part
        store_parts(outs[2:], start, total)
        start += total.shape[1]


def mlp_backward_kernel(packed, d_ref, gate_ref, up_ref, *refs):
    outs = refs[-6:]
    units = outs[0].shape[1] // 2
    d_mlp_core(weight_views(refs, packed), d_ref, (gate_ref, up_ref), units, outs, None)


def mlp_both_kernel(packed, rows, offset_ref, all_ref, x_ref, *refs):
    sorted_ref, hidden_ref = refs[-8:-6]
    outs = refs[-6:]
    units = outs[0].shape[1] // 2
    for i in range(sorted_ref.shape[0] // rows):
        start = pl.multiple_of(offset_ref[i], rows)
        sorted_ref[i * rows : (i + 1) * rows, :] = all_ref[pl.ds(start, rows), :]
    d_mlp_core(weight_views(refs, packed), sorted_ref, (x_ref,), units, outs, hidden_ref)


def weight_specs(layer, mats):
    specs = []
    for m in mats:
        if len(m.shape) == 4:
            specs.append(pl.BlockSpec((m.shape[0] // 2,) + m.shape[1:], lambda i: (layer, 0, 0, 0)))
        else:
            specs.append(pl.BlockSpec((None,) + m.shape[1:], lambda i: (layer, 0, 0)))
    return specs


def part_shapes(rows, width):
    return [jax.ShapeDtypeStruct((rows // 4, width), f32)] + [
        jax.ShapeDtypeStruct((rows // 4, width), bf16)
    ] * 3


def mlp_forward(layer, tokens, mats, units, pins=()):
    rows, width = tokens.shape
    out_shape = [
        jax.ShapeDtypeStruct((rows, 2 * units), f32),
        jax.ShapeDtypeStruct((rows, 2 * units), f32),
        jax.ShapeDtypeStruct((rows, 2 * units), bf16),
    ] + part_shapes(rows, width)
    return call(
        lambda *refs: mlp_forward_kernel(len(mats) == 2, *refs),
        out_shape,
        [VMEM] + weight_specs(layer, mats),
        (tokens, *mats),
        pins,
        12 * rows * width * units,
        grid=(1,),
    )


def mlp_down(layer, offsets, hiddens, mats, width, pins=()):
    rows = sum(h.shape[0] for h in hiddens)
    own = rows // offsets.shape[0]
    return call(
        lambda *refs: mlp_down_kernel(len(mats) == 2, own, *refs),
        [jax.ShapeDtypeStruct((rows, width), bf16)],
        [SMEM] + [VMEM] * len(hiddens) + weight_specs(layer, mats),
        (offsets * own, *hiddens, *mats),
        pins,
        2 * rows * width * hiddens[0].shape[1],
        grid=(1,),
    )[0]


def mlp_backward(layer, d_tokens, gate, up, mats, units, pins=()):
    rows, width = d_tokens.shape
    out_shape = [jax.ShapeDtypeStruct((rows, 2 * units), bf16)] * 2 + part_shapes(rows, width)
    return call(
        lambda *refs: mlp_backward_kernel(len(mats) == 2, *refs),
        out_shape,
        [VMEM] * 3 + weight_specs(layer, mats),
        (d_tokens, gate, up, *mats),
        pins,
        12 * rows * width * units,
        grid=(1,),
    )


def mlp_both(layer, offsets, d_all, tokens, mats, units, own, pins=()):
    rows, width = tokens.shape
    out_shape = [jax.ShapeDtypeStruct((rows, width), bf16)]
    out_shape += [jax.ShapeDtypeStruct((rows, 2 * units), bf16)] * 3 + part_shapes(rows, width)
    return call(
        lambda *refs: mlp_both_kernel(len(mats) == 2, own, *refs),
        out_shape,
        [SMEM, VMEM, VMEM] + weight_specs(layer, mats),
        (offsets * own, d_all, tokens, *mats),
        pins,
        20 * rows * width * units,
        grid=(1,),
    )


def unit_grads_kernel(groups, *refs):
    outs = refs[-2:]
    units = refs[2].shape[1] // 2
    for half, out_ref in enumerate(outs):
        place = slice(half * units, (half + 1) * units)
        totals = [None, None, None]
        for g in range(groups):
            x_ref, d_ref, d_gate_ref, d_up_ref, hidden_ref = refs[g * 5 : g * 5 + 5]
            x, d = x_ref[...], d_ref[...]
            parts = (
                dot_tn(x, d_gate_ref[:, place]),
                dot_tn(x, d_up_ref[:, place]),
                dot_tn(hidden_ref[:, place], d),
            )
            totals = [p if t is None else t + p for t, p in zip(totals, parts)]
        for i in range(3):
            out_ref[0, i] = totals[i].astype(bf16)


def unit_grads(n, inputs, pins=()):
    rows, width = inputs[0][0].shape
    units = inputs[0][2].shape[1] // 2
    cols = width // n
    if cols % LANES:
        made = []
        for place in (slice(0, units), slice(units, 2 * units)):
            totals = [0.0, 0.0, 0.0]
            for x, d, d_gate, d_up, hidden in inputs:
                totals[0] += dot_tn(x, d_gate[:, place]).reshape(n, cols, units)
                totals[1] += dot_tn(x, d_up[:, place]).reshape(n, cols, units)
                totals[2] += dot_tn(hidden[:, place], d).reshape(units, n, cols).transpose(1, 0, 2)
            made.append(jnp.stack(totals, axis=1).astype(bf16))
        return made
    specs, operands = [], []
    for group in inputs:
        for place, array in enumerate(group):
            operands.append(array)
            if place < 2:
                specs.append(pl.BlockSpec((rows, cols), lambda j: (0, j)))
            else:
                specs.append(pl.BlockSpec(array.shape, lambda j: (0, 0)))
    return call(
        lambda *refs: unit_grads_kernel(len(inputs), *refs),
        [jax.ShapeDtypeStruct((n, 3, cols, units), bf16)] * 2,
        specs,
        operands,
        pins,
        12 * len(inputs) * rows * width * units,
        out_specs=[pl.BlockSpec((1, 3, cols, units), lambda j: (j, 0, 0, 0))] * 2,
        grid=(n,),
    )


def add_kernel(kept_ref, got_ref, *refs):
    refs[-1][...] = (kept_ref[...].astype(f32) + got_ref[...].astype(f32)).astype(bf16)


def core_sum(layer, kept, got, into, pins=()):
    n = kept.shape[0]
    if kept.shape[3] % LANES:
        made = (kept.astype(f32) + got.astype(f32)).astype(bf16)
        return made if into is None else jnp.concatenate([made, into], axis=0)
    block = (n // 2,) + kept.shape[1:]
    return call(
        add_kernel,
        [jax.ShapeDtypeStruct((2 * n,) + kept.shape[1:], bf16)],
        [pl.BlockSpec(block, lambda j: (j, 0, 0, 0))] * 2,
        (kept, got),
        ([] if into is None else [into]) + list(pins),
        0,
        out_specs=[pl.BlockSpec(block, lambda j: (2 * layer + j, 0, 0, 0))],
        grid=(2,),
        aliases={} if into is None else {2: 0},
    )[0]


def pack_kernel(gate_ref, up_ref, down_ref, *refs):
    out_ref = refs[-1]
    _, _, cols, units = out_ref.shape
    for i in range(out_ref.shape[0]):
        place = slice(i * units, (i + 1) * units)
        out_ref[i, 0] = gate_ref[:, place]
        out_ref[i, 1] = up_ref[:, place]
        out_ref[i, 2] = down_ref[place, :]


def unpack_kernel(in_ref, gate_w_ref, up_w_ref, *refs):
    gate_ref, up_ref, down_ref, sums_ref = refs[-4:]
    _, _, cols, units = in_ref.shape
    total = jnp.zeros(sums_ref.shape, f32)
    for i in range(in_ref.shape[0]):
        place = slice(i * units, (i + 1) * units)
        gate, up = in_ref[i, 0].astype(f32), in_ref[i, 1].astype(f32)
        gate_ref[:, place] = gate
        up_ref[:, place] = up
        down_ref[place, :] = in_ref[i, 2].astype(f32)
        both = gate_w_ref[:, place].astype(f32) * gate + up_w_ref[:, place].astype(f32) * up
        for lane in range(0, units, LANES):
            total = total + both[:, lane : lane + LANES]

    @pl.when(pl.program_id(0) == 0)
    def _():
        sums_ref[...] = total

    @pl.when(pl.program_id(0) > 0)
    def _():
        sums_ref[...] += total


def packing_specs(cols, units, steps):
    rows = pl.BlockSpec((cols, steps * units), lambda i: (0, i))
    columns = pl.BlockSpec((steps * units, cols), lambda i: (i, 0))
    packed = pl.BlockSpec((steps, 3, cols, units), lambda i: (i, 0, 0, 0))
    return [rows, rows, columns], packed


def packed_units(gate, up, down, pieces, pins):
    cols, units = gate.shape[0], gate.shape[1] // pieces
    specs, packed = packing_specs(cols, units, 4)
    return call(
        pack_kernel,
        [jax.ShapeDtypeStruct((pieces, 3, cols, units), gate.dtype)],
        specs,
        (gate, up, down),
        pins,
        0,
        out_specs=[packed],
        grid=(pieces // 4,),
    )[0]


def unpacked_units(packed_array, gate_w, up_w, pins):
    pieces, _, cols, units = packed_array.shape
    specs, packed = packing_specs(cols, units, 4)
    return call(
        unpack_kernel,
        [
            jax.ShapeDtypeStruct((cols, pieces * units), f32),
            jax.ShapeDtypeStruct((cols, pieces * units), f32),
            jax.ShapeDtypeStruct((pieces * units, cols), f32),
            jax.ShapeDtypeStruct((cols, LANES), f32),
        ],
        [packed] + specs[:2],
        (packed_array, gate_w, up_w),
        pins,
        0,
        out_specs=specs + [pl.BlockSpec((cols, LANES), lambda i: (0, 0))],
        grid=(pieces // 4,),
    )


def on_device(
    tokens, cotangent, attn_gain, w_query, w_key, w_value, w_out, mlp_gain, w_gate, w_up, w_down
):
    plane = lax.axis_index("pipe")
    core = lax.axis_index("tensor")
    place = lax.axis_index("dp")
    n = lax.axis_size("dp")
    first = plane == 0
    seq_len, width = tokens.shape
    own_cols = width // n
    own = seq_len // 4
    q_width = w_query.shape[2] // 2
    kv_width = w_key.shape[2] // 2
    starts = [
        (2 * c + p) * own
        for c, p in ((core, plane), (core, 1 - plane), (1 - core, plane), (1 - core, 1 - plane))
    ]

    def own_rows(rows):
        return lax.dynamic_slice_in_dim(rows, starts[0], own, 0)

    def relative(rows):
        return jnp.concatenate(
            [lax.dynamic_slice_in_dim(rows, start, own, 0) for start in starts], axis=0
        )

    def natural(rows):
        out = jnp.zeros_like(rows)
        for i, start in enumerate(starts):
            out = lax.dynamic_update_slice_in_dim(out, rows[i * own : (i + 1) * own], start, 0)
        return out

    def halves(matrix, axis):
        return jnp.split(matrix, 2, axis=axis)

    units = w_gate.shape[2] // (2 * n)
    by_blocks = own_cols % LANES == 0 and units == own_cols and n == 8
    block_cols = own_cols if by_blocks else width
    gains = jnp.concatenate([attn_gain, mlp_gain], axis=0)
    packed = [
        jnp.concatenate([q, k, v, o.T], axis=1)
        for q, k, v, o in zip(
            halves(w_query[0], 1), halves(w_key[0], 1), halves(w_value[0], 1), halves(w_out[0], 0)
        )
    ]
    if by_blocks:
        row = jnp.pad(gains.reshape(1, -1), ((0, 15), (0, packed[0].shape[1] - 2 * own_cols)))
        packed = [jnp.concatenate([part, row], axis=0) for part in packed]
    got = to_plane(jnp.where(first, packed[1], packed[0]))
    local = [jnp.where(first, packed[0], got), jnp.where(first, got, packed[1])]
    own_cot = own_rows(cotangent)
    cot_all = lax.all_gather(own_cot, ("dp", "pipe"), axis=0, tiled=True)
    owners = [
        jnp.stack(
            [
                (place ^ (2 * k + j % 2)) * 2 + (plane ^ (j // 2))
                for j in range(4)
                for k in group
            ]
        )
        for group in column_groups()
    ]
    both = ("pipe", "dp")

    if by_blocks:
        attn_blocks = [
            [lax.all_gather(after(local[0], [cot_all]), "dp", axis=0)],
            [lax.all_gather(local[1], "dp", axis=0)],
        ]
        offsets = jnp.arange(n, dtype=jnp.int32) * own_cols
        packed_weights = packed_units(w_gate[0], w_up[0], w_down[0], 2 * n, [])
        packed_weights = after(packed_weights, local)
        mats = [lax.all_to_all(packed_weights, both, 0, 0, tiled=True)]
    else:
        other_gains = to_plane(gains)
        local_gains = [jnp.where(first, gains, other_gains), jnp.where(first, other_gains, gains)]
        attn_blocks = [
            [
                lax.all_gather(block, "dp", axis=0, tiled=True),
                lax.all_gather(gain, "dp", axis=1, tiled=True),
            ]
            for block, gain in zip(local, local_gains)
        ]
        offsets = jnp.zeros((1,), jnp.int32)
        down_both = lax.all_to_all(w_down[0], both, 0, 0, tiled=True).reshape(2, n, units, own_cols)
        mats = [
            lax.all_to_all(w_gate[0], both, 1, 0, tiled=True).reshape(2, width, units),
            lax.all_to_all(w_up[0], both, 1, 0, tiled=True).reshape(2, width, units),
            down_both.transpose(0, 2, 1, 3).reshape(2, units, width),
        ]
    mats = mats + [to_core(m) for m in mats]

    positions = jnp.concatenate([start + jnp.arange(own, dtype=jnp.int32) for start in starts])
    causal = positions[None, :] <= positions[:, None]
    tables = rope_tables(positions) + (jnp.where(causal, 0.0, -1e30).astype(f32),)

    def attention(layer, layer_in, pins=()):
        keep, send, q_rot, kv, mixed, xn_own, gains = attend_forward(
            offsets, layer_in, tables, attn_blocks[layer], q_width, block_cols, pins
        )
        middle = layer_in[:own].astype(f32) + sum_four(keep, send)
        xn_two = gather_tokens(normed(middle, gains[1:2]).astype(bf16))
        return xn_two, middle, (gains, xn_own, q_rot, kv, mixed)

    def d_attention(layer, d_middle, layer_in, kept, pins=()):
        gains, xn_own, q_rot, kv, mixed = kept
        keep, send, d_qkv = attend_backward(
            offsets,
            gather_four(d_middle.astype(bf16)),
            q_rot,
            kv,
            tables,
            attn_blocks[layer],
            block_cols,
            pins,
        )
        d_xn_one = sum_four(keep, send)
        _, norm_pull = jax.vjp(lambda v: normed(v, gains[0:1]), layer_in[:own].astype(f32))
        return d_middle + norm_pull(d_xn_one)[0], d_qkv

    def d_norm(upstream, d_xn_two, middle, gains):
        _, norm_pull = jax.vjp(lambda v: normed(v, gains[1:2]), middle)
        return upstream.astype(f32) + norm_pull(d_xn_two)[0]

    def grad_inputs(xs, d_tokens, d_units, hiddens):
        return [
            (x, d, du[0], du[1], h) for x, d, du, h in zip(xs, d_tokens, d_units, hiddens)
        ]

    def dp_all(block, axis):
        return lax.all_gather(block, "dp", axis=axis, tiled=True)

    in_first = relative(tokens)
    xn_first, middle_first, kept_first = attention(0, in_first)
    units_first = [mlp_forward(0, x, mats, units) for x in xn_first]
    first_out = (middle_first + sum_tokens([r[3:] for r in units_first])).astype(bf16)
    in_second = gather_four(first_out)
    xn_second, middle_second, kept_second = attention(1, in_second)
    units_second = [
        mlp_both(1, owner, cot_all, x, mats, units, own) for owner, x in zip(owners, xn_second)
    ]
    cot_sorted = [r[0] for r in units_second]
    hidden_second = [r[1] for r in units_second]
    d_units_second = [r[2:] for r in units_second]
    d_middle_second = d_norm(
        own_cot, sum_tokens([d[2:] for d in d_units_second]), middle_second, kept_second[0]
    )
    mixed_all = dp_all(jnp.stack([kept_first[4], kept_second[4]]), 1)
    d_second, d_qkv_second = d_attention(
        1, d_middle_second, in_second, kept_second, [mixed_all]
    )
    d_second = d_second.astype(bf16)
    d_qkv_second_all = dp_all(d_qkv_second, 0)
    d_all = gather_tokens(d_second)
    made, sent = unit_grads(
        n, grad_inputs(xn_second, cot_sorted, d_units_second, hidden_second), [d_second]
    )
    packed_grads = core_sum(1, made, to_core(sent), None)
    relative_owners = [
        (j // 2) * n + (place ^ (2 * k + j % 2))
        for group in column_groups()
        for j in range(4)
        for k in group
    ]
    partial = mlp_down(1, jnp.stack(relative_owners), hidden_second, mats, width, [d_second])
    half = partial.shape[0] // 2
    partial = partial[:half].astype(f32) + to_plane(partial[half:]).astype(f32)
    partial = lax.psum_scatter(partial.astype(bf16), "dp", scatter_dimension=0, tiled=True)
    second_out = (middle_second + partial.astype(f32)).astype(bf16)
    d_units_first = [
        mlp_backward(0, d, *r[:2], mats, units, [d_qkv_second_all, packed_grads])
        for d, r in zip(d_all, units_first)
    ]
    made, sent = unit_grads(
        n, grad_inputs(xn_first, d_all, d_units_first, [r[2] for r in units_first])
    )
    d_middle_first = d_norm(
        d_second, sum_tokens([d[2:] for d in d_units_first]), middle_first, kept_first[0]
    )
    packed_grads = core_sum(0, made, to_core(sent), packed_grads, [d_middle_first])
    def column_rows(blocks):
        count = len(blocks)
        rows = jnp.concatenate(blocks).reshape(count * own, n, own_cols)
        return lax.all_to_all(rows, "dp", 1, 0).reshape(1, n, count, own, own_cols)

    def all_rows(columns):
        rows = gather_four(columns).transpose(2, 1, 0, 3, 4)
        return rows.reshape(rows.shape[0], n * seq_len, own_cols)

    columns = column_rows(
        [kept_first[1], d_middle_first.astype(bf16), kept_second[1], d_middle_second.astype(bf16)]
    )
    d_first, d_qkv_first = d_attention(
        0, d_middle_first, in_first, kept_first, [columns, partial]
    )
    d_qkv_all = [dp_all(d_qkv_first, 0), d_qkv_second_all]
    columns = all_rows(after(columns, [d_qkv_first]))

    def attention_grads(layer, d_qkv):
        return jnp.concatenate(
            [
                dot_tn(columns[2 * layer], d_qkv),
                dot_tn(columns[2 * layer + 1], mixed_all[layer]),
            ],
            axis=1,
        ).astype(bf16)

    small_first = attention_grads(0, d_qkv_all[0])
    small_second = attention_grads(1, d_qkv_all[1])
    small_own = jnp.where(first, small_first, small_second)
    small_got = to_plane(jnp.where(first, small_second, small_first))
    small = [
        jnp.where(first, small_own, small_got).astype(f32),
        jnp.where(first, small_got, small_own).astype(f32),
    ]
    def joined(start, size):
        return jnp.concatenate([part[:, start : start + size] for part in small], axis=1)

    grad_query = joined(0, q_width)
    grad_key = joined(q_width, kv_width)
    grad_value = joined(q_width + kv_width, kv_width)
    grad_out = joined(q_width + 2 * kv_width, q_width).T
    packed_grads = lax.all_to_all(
        packed_grads, both, 0, 0, tiled=True
    )
    if by_blocks:
        grad_gate, grad_up, grad_down, unit_sums = unpacked_units(
            packed_grads, w_gate[0], w_up[0], [second_out]
        )
        unit_sums = jnp.sum(unit_sums, axis=1)
    else:
        parts = [packed_grads[:, i].astype(f32) for i in range(3)]
        grad_gate, grad_up = [part.transpose(1, 0, 2).reshape(own_cols, -1) for part in parts[:2]]
        grad_down = parts[2].reshape(-1, own_cols)
        unit_sums = jnp.sum(
            w_gate[0].astype(f32) * grad_gate + w_up[0].astype(f32) * grad_up, axis=1
        )
    def row_sums(pairs):
        return sum(jnp.sum(w[0].astype(f32) * grad, axis=1) for w, grad in pairs)

    attn_sums = row_sums(((w_query, grad_query), (w_key, grad_key), (w_value, grad_value)))
    gain_sums = jnp.stack([attn_sums, unit_sums])
    gain_sums = gain_sums + to_core(gain_sums)
    gain_grads = gain_sums / gains.astype(f32)
    activations = natural(jnp.where(first, in_second, gather_four(second_out)))
    input_grads = natural(
        jnp.where(first, gather_four(d_first), gather_four(d_second).astype(f32))
    )
    return (
        activations[None],
        input_grads[None],
        gain_grads[0][None],
        grad_query[None],
        grad_key[None],
        grad_value[None],
        grad_out[None],
        gain_grads[1][None],
        grad_gate[None],
        grad_up[None],
        grad_down[None],
    )


def solution(mesh):
    token_spec = P("dp", None)
    gain_spec = P("pipe", "dp")
    row_spec = P("pipe", "dp", "tensor")
    col_spec = P("pipe", "tensor", "dp")
    in_specs = (
        token_spec,
        token_spec,
        gain_spec,
        row_spec,
        row_spec,
        row_spec,
        col_spec,
        gain_spec,
        row_spec,
        row_spec,
        col_spec,
    )
    out_specs = (
        P("pipe", "dp", None),
        P("pipe", "dp", None),
        gain_spec,
        row_spec,
        row_spec,
        row_spec,
        col_spec,
        gain_spec,
        row_spec,
        row_spec,
        col_spec,
    )
    return jax.shard_map(
        on_device, mesh=mesh, in_specs=in_specs, out_specs=out_specs, check_vma=False
    )
```
